768 devices in a mesh: expert: 4 (over x), tensor: 16 (over y, core), dp: 12 (over z).
Axes of the slice: x: 4, y: 8, z: 12, core: 2. Of those that a mesh axis runs over, the one named last changes fastest.
Arguments:
- grad_out: bfloat16 [12, 1024, 2048], P('dp', 'expert', 'tensor'), may hold values from -6 to 6
- routes: int32 [12, 1024, 8], P('dp', 'expert'), may hold values from 0 to 63, all different within a row; in each aligned block of 256 rows (0 to 255, 256 to 511, ..., all dimensions but the last counted through in order) at most 64 rows name the same one
- gates: bfloat16 [12, 1024, 8], P('dp', 'expert'), may hold values from 0.019897461 to 0.5
- hidden: bfloat16 [64, 3072, 768], P('expert', 'dp'), may hold values from -6 to 6
- w_down: bfloat16 [64, 768, 2048], P('expert', None, 'tensor'), may hold values from -0.21875 to 0.21875
Outputs:
- grad_hidden: bfloat16 [64, 3072, 768], P('expert', ('dp', 'tensor'))
- grad_weight: bfloat16 [64, 768, 2048], P('expert', 'dp', 'tensor')
- grad_gates: float32 [12, 1024, 8], P('dp', 'expert')
The draws below stay inside these ranges and needn't reach their ends.
Inputs may be any that keep to these rules, and one draw needn't show every extreme that they name: `routes`: among the 256 tokens of one block, no expert is named by more than 64 pairs; some expert is named by exactly 64. A token names 8 different experts.
All inputs are finite; a program needn't handle non-finite values.
Results may differ from the reference program's by a relative error of at most 0.023.
Values may be sent and summed in bfloat16 or wider, within the bound.
A program may use at most 64 MiB of HBM per device.

```python
import math
import jax
import jax.numpy as jnp
import numpy as np
from jax import lax

D = 2048
H = 768
TOP = 8
TOK_GRP = 256
EXPERTS = 64
CAP = 64
SLOTS = 256
TOKS = 1024
N_EXPERT = 4
N_TENSOR = 16
N_DP = 12


def strengthened(values, stream_key, source, target, shards_of, factor):
    def block_of(position):
        return (jnp.arange(values.shape[position]) // (values.shape[position] // shards_of)).reshape((-1,) + (1,) * (values.ndim - 1 - position))

    first = jax.random.permutation(stream_key, shards_of)[block_of(target)]
    far = (block_of(target) + shards_of // 2) % shards_of
    return jnp.where((block_of(source) == first) | (block_of(source) == far), factor * values, values)


def level_of(stream_key, dims, shards, least, top_value):
    loudness, own = 1.0, jax.random.fold_in(stream_key, 6)
    for axis_at, shards_of in shards:
        heights = jnp.exp(jax.random.uniform(jax.random.fold_in(own, axis_at), (shards_of,), jnp.float32, least / len(shards), top_value / len(shards)))
        loudness = loudness * jnp.repeat(heights, dims[axis_at] // shards_of).reshape([-1 if axis == axis_at else 1 for axis in range(len(dims))])
    return loudness


def assign_block(stream_key, own, number, rows, number_of, top, bound, skew):
    order = jax.random.permutation(stream_key, number_of)
    heavy_load, common = load_shares(number_of, rows * top, bound, skew, True), load_shares(number_of, rows * top, bound, skew, False)
    places = jnp.arange(number_of)

    def named(sizes, turn):
        used = int((sizes > 0).sum())
        fixed = max(1, used // 4)
        passed = fixed + (places - fixed + turn * (used - fixed)) % max(1, number_of - fixed)
        return jnp.zeros((number_of,), jnp.int32).at[order[jnp.where(places < fixed, places, passed)]].set(jnp.asarray(sizes, jnp.int32))

    sizes = jnp.where(number % 4 == 0, named(heavy_load, number // 4), named(common, number - number // 4 - 1))
    mixed = jax.random.permutation(jax.random.fold_in(own, 3), number_of)
    source_of, sink = mixed[0:number_of // 2 * 2:2], mixed[1:number_of // 2 * 2:2]
    slack = jnp.minimum(sizes[source_of] - 1, bound - sizes[sink]) // 2
    slack = jnp.where((source_of == order[0]) | (sink == order[0]) | (sizes[sink] == 0), 0, jnp.maximum(slack, 0))
    passed = jax.random.randint(jax.random.fold_in(own, 4), (number_of // 2,), 0, 1 << 20) % (slack + 1)
    sizes = sizes.at[source_of].add(-passed).at[sink].add(passed)
    labels = jnp.searchsorted(jnp.cumsum(sizes), jnp.arange(rows * top), side="right").astype(jnp.int32)
    listing = labels.reshape(top, rows).T
    listing = listing[jax.random.permutation(jax.random.fold_in(own, 1), rows)]
    turn = jax.random.randint(jax.random.fold_in(own, 2), (rows, 1), 0, top)
    return jnp.take_along_axis(listing, (jnp.arange(top)[None, :] + turn) % top, axis=1)


def load_shares(amount, total, limit, lean, full):
    portions = [(1 << 20) // math.isqrt(grade ** lean) + 1 for grade in range(1, amount + 1)]
    largest = limit if full else min(limit, max(-(-total // amount), total * portions[0] // sum(portions)))
    least = 1 if total - largest >= amount - 1 else 0
    counts, surplus = [largest] + [least] * (amount - 1), total - largest - least * (amount - 1)
    while surplus > 0:
        movable = [i for i in range(1, amount) if counts[i] < largest] or [i for i in range(1, amount) if counts[i] < limit]
        whole, remaining = sum([portions[i] for i in movable]), surplus
        for i in movable:
            more = min(limit - counts[i], max(1, remaining * portions[i] // whole), surplus)
            counts[i] = counts[i] + more
            surplus = surplus - more
    return np.array(counts)


def noise(key, dims, width, limit, pieces=(), held_as=jnp.bfloat16):
    factor_of = level_of(key, dims, pieces, -0.22, 0.18) if pieces else 1.0
    values = jax.random.normal(key, dims, jnp.float32) * width * factor_of
    return jnp.minimum(jnp.maximum(values, -limit), limit).astype(held_as)


def noise_with(own_key, shape, spread, most, split, heavy, held_as=jnp.bfloat16):
    entries = spread * jax.random.normal(own_key, shape, jnp.float32)
    if split:
        entries = entries * level_of(own_key, shape, split, -0.22, 0.18)
    return jnp.clip(strengthened(entries, jax.random.fold_in(own_key, 3), *heavy), -most, most).astype(held_as)


def setup_inputs(seed: int = 0) -> dict:
    arg_keys = jax.random.split(jax.random.key(seed), 6)
    grad_out = noise(arg_keys[0], (N_DP, TOKS, D), 1.0, 6.0, ((0, 12), (1, 4), (2, 16)))
    routes_keys = jax.random.split(jax.random.fold_in(arg_keys[1], 1), N_DP * TOKS // TOK_GRP)
    routes_turns = jax.random.permutation(jax.random.fold_in(arg_keys[1], 3), N_DP * TOKS // TOK_GRP)
    routes = jax.vmap(lambda own, number: assign_block(jax.random.fold_in(arg_keys[1], 2), own, number, TOK_GRP, EXPERTS, TOP, CAP, 2))(routes_keys, routes_turns).reshape((N_DP, TOKS, TOP))
    gates = jnp.clip(jnp.exp(math.log(0.5) - 3.224016 * jax.random.uniform(arg_keys[2], (N_DP, TOKS, TOP), jnp.float32) ** level_of(arg_keys[2], (N_DP, TOKS, TOP), ((0, 12), (1, 4)), -0.2, 0.2)), 0.019897461, 0.5).astype(jnp.bfloat16)
    hidden = noise_with(arg_keys[3], (EXPERTS, N_DP * SLOTS, H), 1.0, 6.0, ((0, 4), (1, 12)), (1, 2, 12, 2.0))
    w_down = noise(arg_keys[4], (EXPERTS, H, D), H ** -0.5, 0.21875, ((0, 4), (2, 16)))
    return {"grad_out": grad_out, "routes": routes, "gates": gates, "hidden": hidden, "w_down": w_down}


def reference(grad_out, routes, gates, hidden, w_down):
    blocks = N_DP * N_EXPERT
    slots = N_EXPERT * CAP
    total_rows = N_DP * slots
    width_part = D // N_TENSOR
    chosen = routes.reshape(blocks, TOK_GRP * TOP)
    expert_hot = (chosen[:, :, None] == jnp.arange(EXPERTS, dtype=jnp.int32)[None, None, :]).astype(jnp.int32)
    earlier = jnp.cumsum(expert_hot, 1) - expert_hot
    rank = jnp.sum(earlier * expert_hot, 2).astype(jnp.int32)
    block_ids = jnp.arange(blocks, dtype=jnp.int32)
    base = (block_ids // N_EXPERT) * slots + (block_ids % N_EXPERT) * CAP
    slot_row = (base[:, None] + rank).astype(jnp.int32)
    token_ids = (block_ids[:, None] * TOK_GRP + jnp.arange(TOK_GRP * TOP, dtype=jnp.int32)[None, :] // TOP).astype(jnp.int32)
    flat_expert = chosen.reshape(-1)
    flat_row = slot_row.reshape(-1)
    source = jnp.full((EXPERTS, total_rows), -1, jnp.int32).at[flat_expert, flat_row].set(token_ids.reshape(-1))
    weight_table = jnp.zeros((EXPERTS, total_rows), jnp.float32).at[flat_expert, flat_row].set(gates.reshape(-1).astype(jnp.float32))
    dy_all = grad_out.reshape(-1, D)

    def per_expert(items):
        src, gate_col, hid, weight = items
        dy = jnp.where((src >= 0)[:, None], dy_all[jnp.maximum(src, 0)], jnp.zeros((), jnp.bfloat16))
        dyf = dy.astype(jnp.float32)
        scaled = (gate_col[:, None] * dyf).astype(jnp.bfloat16)
        sf = scaled.astype(jnp.float32)
        hf = hid.astype(jnp.float32)
        wf = weight.astype(jnp.float32)
        wparts = jnp.einsum("psh,psd->phd", hf.reshape(N_DP, slots, H), sf.reshape(N_DP, slots, D))
        wparts = lax.optimization_barrier(wparts.astype(jnp.bfloat16)).astype(jnp.float32)
        grad_w = jnp.sum(wparts, 0).astype(jnp.bfloat16)
        hparts = jnp.einsum("rtd,htd->trh", sf.reshape(total_rows, N_TENSOR, width_part), wf.reshape(H, N_TENSOR, width_part))
        hparts = lax.optimization_barrier(hparts.astype(jnp.bfloat16)).astype(jnp.float32)
        grad_h = jnp.sum(hparts, 0).astype(jnp.bfloat16)
        output = jnp.dot(hf, wf, preferred_element_type=jnp.float32)
        slot_gate = jnp.sum(dyf * output, 1)
        return grad_h, grad_w, slot_gate

    grad_hidden, grad_weight, slot_gate = lax.map(per_expert, (source, weight_table, hidden, w_down))
    grad_gates = slot_gate[flat_expert, flat_row].reshape(N_DP, N_EXPERT * TOK_GRP, TOP)
    return grad_hidden, grad_weight, grad_gates
```

```python
import functools
import math

import jax
import jax.numpy as jnp
from jax import lax
from jax.experimental import pallas as pl
from jax.experimental.pallas import tpu as pltpu
from jax.sharding import PartitionSpec as P

MESH = pl.DeviceIdType.MESH
BF = jnp.bfloat16
F32 = jnp.float32


def mod(a, n):
    return lax.rem(a, jnp.int32(n))


def div(a, n):
    return lax.div(a, jnp.int32(n))


def kernel(
    nx, ny, nz, groups,
    go_in, routes, gates, hid_in, w_in,
    gh_out, gw_out, gg_out,
    hid, w2, go_all, rg_send, rg, dyh, sc, mh, mg, gcol,
    ty, tz, ry, rz, gall, sgx, gsc,
    hid_sem, wl_sem, ws_sem, wr_sem, go_l, gox_s, gox_r, goc_s, goc_r, rg_s, rg_r,
    ys_sem, yr_sem, zs_sem, zr_sem, ga_s, ga_r, sg_s, sg_r,
):
    top, toks = routes.shape
    width = go_in.shape[1]
    experts, _, _, q, h = hid.shape
    per = experts // groups
    cap = 2 * ny * q // nx
    yb = ny // nx
    half = yb * q
    hz = h // nz
    lanes = ny * q
    x = lax.axis_index("expert")
    t = lax.axis_index("tensor")
    z = lax.axis_index("dp")
    y = div(t, 2)
    c = mod(t, 2)
    peer_c = 1 - c

    def dev(xx, yy, cc, zz):
        return {"expert": xx, "tensor": yy * 2 + cc, "dp": zz}

    def xat(dx):
        return mod(x + dx, nx)

    def yat(dy):
        return mod(y + dy, ny)

    def zat(dz):
        return mod(z + dz, nz)

    peer = dev(x, y, peer_c, z)

    def remote(src, dst, ssem, rsem, to):
        return pltpu.make_async_remote_copy(
            src_ref=src, dst_ref=dst, send_sem=ssem, recv_sem=rsem,
            device_id=to, device_id_type=MESH,
        )

    barrier = pltpu.get_barrier_semaphore()
    partners = [peer]
    partners += [dev(xat(dx), y, mod(c + r, 2), z) for dx in range(1, nx) for r in (0, 1)]
    partners += [dev(x, yat(dy), c, z) for dy in range(1, ny)]
    partners += [dev(x, y, c, zat(dz)) for dz in sorted({1, nz - 1})]
    for partner in partners:
        pl.semaphore_signal(barrier, inc=1, device_id=partner, device_id_type=MESH)

    mine = pl.ds(pl.multiple_of(c * width, width), width)
    others = pl.ds(pl.multiple_of(peer_c * width, width), width)

    def group(g):
        return pl.ds(g * per, per)

    go_local = pltpu.make_async_copy(go_in, go_all.at[x, :, mine], go_l)
    go_local.start()

    def hid_copy(g):
        return pltpu.make_async_copy(hid_in.at[group(g)], hid.at[group(g)], hid_sem.at[g])

    def w_copy(g):
        return pltpu.make_async_copy(w_in.at[group(g)], w2.at[group(g), :, mine], wl_sem.at[g])

    def w_send(g):
        return remote(w_in.at[group(g)], w2.at[group(g), :, mine], ws_sem.at[g], wr_sem.at[g], peer)

    def w_recv(g):
        place = w2.at[group(g), :, others]
        return remote(place, place, ws_sem.at[g], wr_sem.at[g], peer)

    for g in range(groups):
        w_copy(g).start()
        hid_copy(g).start()

    all_experts = nx * experts
    eidx = lax.broadcasted_iota(jnp.int32, (all_experts, toks), 0)
    hot = jnp.zeros((all_experts, toks), F32)
    weight = jnp.zeros((all_experts, toks), F32)
    gf = gates[...].astype(F32)
    rt = routes[...]
    for k in range(top):
        named = rt[k : k + 1, :] == eidx
        hot = jnp.where(named, 1.0, hot)
        weight = jnp.where(named, gf[k : k + 1, :], weight)
    before = lax.broadcasted_iota(jnp.int32, (toks, toks), 0) < lax.broadcasted_iota(
        jnp.int32, (toks, toks), 1
    )
    rank = jnp.dot(hot.astype(BF), before.astype(F32).astype(BF), preferred_element_type=F32)
    rank = jnp.where(hot > 0.5, rank, -1.0)
    for g in range(nx):
        rg_send[g, 0] = rank[g * experts : (g + 1) * experts]
        rg_send[g, 1] = weight[g * experts : (g + 1) * experts]
    rg[x] = rg_send[x]

    pl.semaphore_wait(barrier, len(partners))

    def gox_send(dx):
        return remote(
            go_in, go_all.at[x, :, mine], gox_s.at[dx], gox_r.at[dx], dev(xat(dx), y, c, z)
        )

    def gox_recv(dx):
        place = go_all.at[xat(nx - dx), :, mine]
        return remote(place, place, gox_s.at[dx], gox_r.at[dx], dev(xat(dx), y, c, z))

    def goc_send(dx):
        src = xat(nx - dx)
        place = go_all.at[src, :, mine]
        return remote(place, place, goc_s.at[dx], goc_r.at[dx], peer)

    def goc_recv(dx):
        place = go_all.at[xat(nx - dx), :, others]
        return remote(place, place, goc_s.at[dx], goc_r.at[dx], peer)

    def rg_copy(dx):
        to = xat(dx)
        return remote(
            rg_send.at[to], rg.at[x], rg_s.at[dx], rg_r.at[dx], dev(to, y, c, z)
        )

    def rg_recv(dx):
        place = rg.at[xat(nx - dx)]
        return remote(place, place, rg_s.at[dx], rg_r.at[dx], dev(xat(dx), y, c, z))

    order = sorted(range(1, nx), key=lambda dx: -min(dx, nx - dx))
    for dx in order:
        gox_send(dx).start()
    for dx in order:
        rg_copy(dx).start()
    go_local.wait()
    goc_send(0).start()
    for g in range(groups):
        w_send(g).start()
    for dx in reversed(order):
        gox_recv(dx).wait_recv()
        goc_send(dx).start()
    for dx in reversed(order):
        rg_recv(dx).wait_recv()
    goc_recv(0).wait_recv()
    for dx in reversed(order):
        goc_recv(dx).wait_recv()

    def chain(n, g, d):
        even = mod(g, 2) if d == 0 else 1 - mod(g, 2)
        return n // 2 - even if n % 2 == 0 else jnp.int32(n // 2)

    def y_chunk(buf, i, g):
        return buf.at[i, group(g)]

    def y_msg(d, k, g, src):
        to = dev(x, yat(1 if d == 0 else ny - 1), c, z)
        return remote(
            src, ry.at[d, k, group(g)], ys_sem.at[d, k, g], yr_sem.at[d, k, g], to
        )

    def z_msg(d, k, g, src):
        to = dev(x, y, c, zat(1 if d == 0 else nz - 1))
        return remote(
            src, rz.at[d, k, group(g)], zs_sem.at[d, k, g], zr_sem.at[d, k, g], to
        )

    def away(at, n, d, steps):
        return mod(at + steps, n) if d == 0 else mod(at + n - steps, n)

    rings = (
        (ny, y, ty, ry, y_msg),
        (nz, z, tz, rz, z_msg),
    )

    slot_full = lax.broadcasted_iota(jnp.int32, (cap, toks), 0).astype(F32)
    row = lax.broadcasted_iota(jnp.int32, (half, toks), 0)
    slot_half = (div(row, q) * (2 * q) + c * q + mod(row, q)).astype(F32)
    own_row = lax.broadcasted_iota(jnp.int32, (q, toks), 0)
    slot_own = (own_row + (mod(y, yb) * (2 * q) + c * q)).astype(F32)
    own_block = div(y, yb)
    tile = 256 if h % 256 == 0 else 128

    def produce(g, _):
        hid_copy(g).wait()
        w_copy(g).wait()
        w_recv(g).wait_recv()

        def dispatch(j, _):
            for e in range(per):
                rk = rg[j, 0, pl.ds(g * per + e, 1), :]
                gt = rg[j, 1, pl.ds(g * per + e, 1), :]
                mh[e * half : (e + 1) * half, :] = jnp.where(rk == slot_half, 1.0, 0.0).astype(BF)
                mg[e * cap : (e + 1) * cap, :] = jnp.where(rk == slot_full, gt, 0.0).astype(BF)
            rows = jnp.dot(mh[...], go_all[j], preferred_element_type=F32).astype(BF)
            scaled = jnp.dot(mg[...], go_all[j, :, mine], preferred_element_type=F32).astype(BF)
            dyh[:, pl.ds(pl.multiple_of(j * half, half), half), :] = rows.reshape(
                per, half, 2 * width
            )
            sc[:, pl.ds(pl.multiple_of(j * cap, cap), cap), :] = scaled.reshape(per, cap, width)
            return 0

        lax.fori_loop(0, nx, dispatch, 0)

        def expert(e, _):
            ee = g * per + e
            own_rank = rg[own_block, 0, pl.ds(ee, 1), :]
            own_gate = rg[own_block, 1, pl.ds(ee, 1), :]
            picked = jnp.sum(jnp.where(own_rank == slot_own, own_gate, 0.0), axis=1, keepdims=True)
            gcol[ee] = jnp.broadcast_to(picked, (q, 128))
            rows = dyh[e]
            part = jnp.zeros((lanes, 128), F32)
            for s in range(0, h, tile):
                u = lax.dot_general(
                    rows, w2[ee, s : s + tile, :], (((1,), (1,)), ((), ())),
                    preferred_element_type=F32,
                )
                hh = hid[ee, :, c, :, s : s + tile].reshape(lanes, tile).astype(F32)
                prod = u * hh
                for i in range(0, tile, 128):
                    part = part + prod[:, i : i + 128]
                ty[:, ee, :, s : s + tile] = u.astype(BF).reshape(ny, q, tile)
            gall[y, pl.ds(ee, 1), :] = jnp.sum(part.T, axis=0, keepdims=True)
            wpart = lax.dot_general(
                hid[ee].reshape(2 * lanes, h), sc[e], (((0,), (0,)), ((), ())),
                preferred_element_type=F32,
            )
            tz[:, ee] = wpart.astype(BF).reshape(nz, hz, width)
            return 0

        lax.fori_loop(0, per, expert, 0)
        for n, at, term, buf, msg in rings:
            for d in (0, 1):
                length = chain(n, g, d)

                @pl.when(length > 0)
                def _():
                    dest = away(at, n, d, length)
                    msg(d, 0, g, term.at[dest, group(g)]).start()

        return 0

    lax.fori_loop(0, groups, produce, 0)

    def ga_send(dy):
        return remote(
            gall.at[y], gall.at[y], ga_s.at[dy], ga_r.at[dy], dev(x, yat(dy), c, z)
        )

    def ga_recv(dy):
        place = gall.at[yat(ny - dy)]
        return remote(place, place, ga_s.at[dy], ga_r.at[dy], dev(x, yat(dy), c, z))

    for dy in range(1, ny):
        ga_send(dy).start()

    offsets = [(dx, r) for dx in range(nx) for r in (0, 1) if dx or r]

    def sg_send(dx, r):
        return remote(
            sgx.at[x, c], sgx.at[x, c], sg_s.at[dx, r], sg_r.at[dx, r],
            dev(xat(dx), y, mod(c + r, 2), z),
        )

    def sg_recv(dx, r):
        place = sgx.at[xat(nx - dx), mod(c + r, 2)]
        return remote(
            place, place, sg_s.at[dx, r], sg_r.at[dx, r], dev(xat(dx), y, mod(c + r, 2), z)
        )

    def sum_gates():
        for dy in range(1, ny):
            ga_recv(dy).wait_recv()
        total = gall[0]
        for i in range(1, ny):
            total = total + gall[i]
        sgx[x, c] = total
        for dx, r in offsets:
            sg_send(dx, r).start()

    def place_gates():
        for dx, r in offsets:
            sg_recv(dx, r).wait_recv()
        for g in range(nx):
            slot = jnp.maximum(rg_send[g, 0], 0.0).astype(jnp.int32)
            lane = (x * yb + div(slot, 2 * q)) * q + mod(slot, q)
            odd = mod(div(slot, q), 2) == 1
            for s in range(0, toks, lanes):
                idx = lane[:, s : s + lanes]
                low = jnp.take_along_axis(sgx[g, 0], idx, axis=1, mode="promise_in_bounds")
                high = jnp.take_along_axis(sgx[g, 1], idx, axis=1, mode="promise_in_bounds")
                gsc[g * experts : (g + 1) * experts, s : s + lanes] = jnp.where(
                    odd[:, s : s + lanes], high, low
                )
        chosen = routes[...]
        out = jnp.zeros((top, toks), F32)
        for e in range(all_experts):
            out = jnp.where(chosen == e, gsc[e : e + 1, :], out)
        gg_out[...] = out

    def add_on(n, at, term, buf, msg, unit):
        k = div(unit, groups) + 1
        g = mod(unit, groups)
        last = n // 2
        for d in (0, 1):
            length = chain(n, g, d)

            @pl.when(k < length)
            def _():
                place = buf.at[d, k - 1, group(g)]
                msg(d, k - 1, g, place).wait_recv()
                dest = away(at, n, d, length - k)
                held = buf[d, k - 1, group(g)].astype(F32) + term[dest, group(g)].astype(F32)
                buf[d, k - 1, group(g)] = held.astype(BF)
                msg(d, k, g, place).start()

        return k == last, g

    def finish(n, at, term, buf, msg, g, store):
        for d in (0, 1):
            length = chain(n, g, d)

            @pl.when(length > 0)
            def _():
                msg(d, length - 1, g, buf.at[d, length - 1, group(g)]).wait_recv()

        total = term[at, group(g)].astype(F32)
        for d in (0, 1):
            length = chain(n, g, d)
            came = buf[d, jnp.maximum(length - 1, 0), group(g)].astype(F32)
            if n == 2:
                came = jnp.where(length > 0, came, 0.0)
            total = total + came
        store(total, g)

    def store_y(total, g):
        scale = gcol[group(g)]
        for s in range(0, h, 128):
            gh_out[group(g), :, s : s + 128] = (total[:, :, s : s + 128] * scale).astype(BF)

    def store_z(total, g):
        gw_out[group(g)] = total.astype(BF)

    yu, zu = (ny // 2) * groups, (nz // 2) * groups
    steps = math.gcd(yu, zu)

    def ring_step(s, _):
        for ring, units, store in ((rings[0], yu, store_y), (rings[1], zu, store_z)):
            for i in range(units // steps):
                final, g = add_on(*ring, s * (units // steps) + i)

                @pl.when(final)
                def _():
                    finish(*ring, g, store)

        pl.when(s == steps // 4)(sum_gates)
        pl.when(s == steps // 2)(place_gates)
        return 0

    lax.fori_loop(0, steps, ring_step, 0)

    def drain(g, _):
        w_send(g).wait_send()
        for n, at, term, buf, msg in rings:
            for d in (0, 1):
                length = chain(n, g, d)
                for k in range(n // 2):

                    @pl.when(k < length)
                    def _():
                        msg(d, k, g, term.at[0, group(g)]).wait_send()

        return 0

    lax.fori_loop(0, groups, drain, 0)
    goc_send(0).wait_send()
    for dx in range(1, nx):
        gox_send(dx).wait_send()
        goc_send(dx).wait_send()
        rg_copy(dx).wait_send()
    for dy in range(1, ny):
        ga_send(dy).wait_send()
    for dx, r in offsets:
        sg_send(dx, r).wait_send()


def on_device(nx, ny, nz, groups, grad_out, routes, gates, hidden, w_down):
    experts, slots, h = hidden.shape
    _, toks, width = grad_out.shape
    top = routes.shape[2]
    q = slots // (2 * ny)
    hz = h // nz
    per = experts // groups
    cap = slots // nx
    half = cap // 2
    ky, kz = max(ny // 2, 1), max(nz // 2, 1)
    dma = pltpu.SemaphoreType.DMA
    vmem = pl.BlockSpec(memory_space=pltpu.VMEM)
    anywhere = pl.BlockSpec(memory_space=pl.ANY)
    gh, gw, gg = pl.pallas_call(
        functools.partial(kernel, nx, ny, nz, groups),
        out_shape=(
            jax.ShapeDtypeStruct((experts, q, h), BF),
            jax.ShapeDtypeStruct((experts, hz, width), BF),
            jax.ShapeDtypeStruct((top, toks), F32),
        ),
        in_specs=[anywhere, vmem, vmem, anywhere, anywhere],
        out_specs=(vmem, vmem, vmem),
        scratch_shapes=[
            pltpu.VMEM((experts, ny, 2, q, h), BF),
            pltpu.VMEM((experts, h, 2 * width), BF),
            pltpu.VMEM((nx, toks, 2 * width), BF),
            pltpu.VMEM((nx, 2, experts, toks), F32),
            pltpu.VMEM((nx, 2, experts, toks), F32),
            pltpu.VMEM((per, ny * q, 2 * width), BF),
            pltpu.VMEM((per, slots, width), BF),
            pltpu.VMEM((per * half, toks), BF),
            pltpu.VMEM((per * cap, toks), BF),
            pltpu.VMEM((experts, q, 128), F32),
            pltpu.VMEM((ny, experts, q, h), BF),
            pltpu.VMEM((nz, experts, hz, width), BF),
            pltpu.VMEM((2, ky, experts, q, h), BF),
            pltpu.VMEM((2, kz, experts, hz, width), BF),
            pltpu.VMEM((ny, experts, ny * q), F32),
            pltpu.VMEM((nx, 2, experts, ny * q), F32),
            pltpu.VMEM((nx * experts, toks), F32),
            dma((groups,)),
            dma((groups,)),
            dma((groups,)),
            dma((groups,)),
            dma,
            dma((nx,)),
            dma((nx,)),
            dma((nx,)),
            dma((nx,)),
            dma((nx,)),
            dma((nx,)),
            dma((2, ky, groups)),
            dma((2, ky, groups)),
            dma((2, kz, groups)),
            dma((2, kz, groups)),
            dma((ny,)),
            dma((ny,)),
            dma((nx, 2)),
            dma((nx, 2)),
        ],
        compiler_params=pltpu.CompilerParams(
            collective_id=0, has_side_effects=True, vmem_limit_bytes=58 * 1024 * 1024
        ),
    )(
        grad_out.reshape(toks, width),
        routes.reshape(toks, top).T,
        gates.reshape(toks, top).T,
        hidden.reshape(experts, ny, 2, q, h),
        w_down,
    )
    return gh, gw, gg.T.reshape(1, toks, top)


def solution(mesh):
    nx, ny, nz = mesh.shape["expert"], mesh.shape["tensor"] // 2, mesh.shape["dp"]
    groups = 4
    placed = (
        P("dp", "expert", "tensor"),
        P("dp", "expert", None),
        P("dp", "expert", None),
        P("expert", "dp", None),
        P("expert", None, "tensor"),
    )
    return jax.shard_map(
        functools.partial(on_device, nx, ny, nz, groups),
        mesh=mesh,
        in_specs=placed,
        out_specs=(
            P("expert", ("dp", "tensor"), None),
            P("expert", "dp", "tensor"),
            P("dp", "expert", None),
        ),
        check_vma=False,
    )
```

```python
import functools
import heapq

import jax
import jax.numpy as jnp
from jax import lax
from jax.experimental import pallas as pl
from jax.experimental.pallas import tpu as pltpu
from jax.sharding import PartitionSpec as P

MESH = pl.DeviceIdType.MESH
BF = jnp.bfloat16
F32 = jnp.float32


def mod(a, n):
    return lax.rem(a, jnp.int32(n))


def div(a, n):
    return lax.div(a, jnp.int32(n))


def timeline(ny, nz, groups):
    size = {0: 8.8 / groups, 1: 5.8 / groups}
    steps = {0: ny // 2, 1: nz // 2}
    work = {"make": 5.4 / groups, "add": 1.6 / groups}
    latency = 1.8
    makes = [(r, g) for g in range(groups) for r in (1, 0)]
    free = {0: 0.0, 1: 0.0}
    ready, order, now, gate = [], [], 0.0, None

    def send(r, k, g, at):
        free[r] = max(free[r], at) + size[r]
        heapq.heappush(ready, (free[r] + latency, r, k + 1, g))

    while makes or ready or gate:
        if gate and gate[0] <= now:
            order.append(("gate", 0, gate[1], 0))
            now += 0.3
            gate = (now + 6.0, gate[1] + 1) if gate[1] < 2 else None
        elif ready and (ready[0][0] <= now or not makes):
            arrived, r, k, g = heapq.heappop(ready)
            now = max(now, arrived) + work["add"]
            order.append(("end" if k == steps[r] else "add", r, k, g))
            if k < steps[r]:
                send(r, k, g, now)
        elif makes:
            r, g = makes.pop(0)
            now += work["make"]
            order.append(("make", r, 0, g))
            send(r, 0, g, now)
            if not makes:
                gate = (now, 0)
        else:
            now = gate[0]
    return order


def kernel(
    nx, ny, nz, groups,
    go_in, routes, gates, hid_in, w_in,
    gh_out, gw_out, gg_out,
    hid, w2, go_all, rg_send, rg, dyh, sc, mh, mg, gcol,
    ty, tz, ry, rz, gall, sgx, gsc, rgf,
    hid_sem, wl_sem, ws_sem, wr_sem, go_l, gox_s, gox_r, goc_s, goc_r, rg_s, rg_r,
    ys_sem, yr_sem, zs_sem, zr_sem, ga_s, ga_r, sg_s, sg_r,
):
    top, toks = routes.shape
    width = go_in.shape[1]
    experts, _, _, q, h = hid.shape
    per = experts // groups
    cap = 2 * ny * q // nx
    yb = ny // nx
    half = yb * q
    hz = h // nz
    lanes = ny * q
    x = lax.axis_index("expert")
    t = lax.axis_index("tensor")
    z = lax.axis_index("dp")
    y = div(t, 2)
    c = mod(t, 2)
    peer_c = 1 - c

    def dev(xx, yy, cc, zz):
        return {"expert": xx, "tensor": yy * 2 + cc, "dp": zz}

    def xat(dx):
        return mod(x + dx, nx)

    def yat(dy):
        return mod(y + dy, ny)

    def zat(dz):
        return mod(z + dz, nz)

    peer = dev(x, y, peer_c, z)

    def remote(src, dst, ssem, rsem, to):
        return pltpu.make_async_remote_copy(
            src_ref=src, dst_ref=dst, send_sem=ssem, recv_sem=rsem,
            device_id=to, device_id_type=MESH,
        )

    barrier = pltpu.get_barrier_semaphore()
    partners = [peer]
    partners += [dev(xat(dx), y, mod(c + r, 2), z) for dx in range(1, nx) for r in (0, 1)]
    partners += [dev(x, yat(dy), c, z) for dy in range(1, ny)]
    partners += [dev(x, y, c, zat(dz)) for dz in sorted({1, nz - 1})]
    for partner in partners:
        pl.semaphore_signal(barrier, inc=1, device_id=partner, device_id_type=MESH)

    mine = pl.ds(pl.multiple_of(c * width, width), width)
    others = pl.ds(pl.multiple_of(peer_c * width, width), width)

    def group(g):
        return pl.ds(g * per, per)

    go_local = pltpu.make_async_copy(go_in, go_all.at[x, :, mine], go_l)
    go_local.start()

    def hid_copy(g):
        return pltpu.make_async_copy(hid_in.at[group(g)], hid.at[group(g)], hid_sem.at[g])

    def w_copy(g):
        return pltpu.make_async_copy(w_in.at[group(g)], w2.at[group(g), :, mine], wl_sem.at[g])

    def w_send(g):
        return remote(w_in.at[group(g)], w2.at[group(g), :, mine], ws_sem.at[g], wr_sem.at[g], peer)

    def w_recv(g):
        place = w2.at[group(g), :, others]
        return remote(place, place, ws_sem.at[g], wr_sem.at[g], peer)

    for g in range(groups):
        w_copy(g).start()
        hid_copy(g).start()

    pl.semaphore_wait(barrier, len(partners))

    def gox_send(dx):
        return remote(
            go_in, go_all.at[x, :, mine], gox_s.at[dx], gox_r.at[dx], dev(xat(dx), y, c, z)
        )

    def gox_recv(dx):
        place = go_all.at[xat(nx - dx), :, mine]
        return remote(place, place, gox_s.at[dx], gox_r.at[dx], dev(xat(dx), y, c, z))

    def goc_send(dx):
        src = xat(nx - dx)
        place = go_all.at[src, :, mine]
        return remote(place, place, goc_s.at[dx], goc_r.at[dx], peer)

    def goc_recv(dx):
        place = go_all.at[xat(nx - dx), :, others]
        return remote(place, place, goc_s.at[dx], goc_r.at[dx], peer)

    def rg_copy(dx):
        to = xat(dx)
        return remote(
            rg_send.at[to], rg.at[x], rg_s.at[dx], rg_r.at[dx], dev(to, y, c, z)
        )

    def rg_recv(dx):
        place = rg.at[xat(nx - dx)]
        return remote(place, place, rg_s.at[dx], rg_r.at[dx], dev(xat(dx), y, c, z))

    order = sorted(range(1, nx), key=lambda dx: -min(dx, nx - dx))
    for dx in order:
        gox_send(dx).start()
    go_local.wait()
    goc_send(0).start()
    for g in range(groups):
        w_send(g).start()

    all_experts = nx * experts
    eidx = lax.broadcasted_iota(jnp.int32, (all_experts, toks), 0)
    hot = jnp.zeros((all_experts, toks), F32)
    weight = jnp.zeros((all_experts, toks), F32)
    gf = gates[...].astype(F32)
    rt = routes[...]
    for k in range(top):
        named = rt[k : k + 1, :] == eidx
        hot = jnp.where(named, 1.0, hot)
        weight = jnp.where(named, gf[k : k + 1, :], weight)
    before = lax.broadcasted_iota(jnp.int32, (toks, toks), 0) < lax.broadcasted_iota(
        jnp.int32, (toks, toks), 1
    )
    rank = jnp.dot(hot.astype(BF), before.astype(F32).astype(BF), preferred_element_type=F32)
    rank = jnp.where(hot > 0.5, rank, -1.0)
    for g in range(nx):
        rg_send[g, 0] = rank[g * experts : (g + 1) * experts].astype(BF)
        rg_send[g, 1] = weight[g * experts : (g + 1) * experts].astype(BF)
    rg[x] = rg_send[x]
    for dx in order:
        rg_copy(dx).start()
    for dx in reversed(order):
        gox_recv(dx).wait_recv()
        goc_send(dx).start()
    for dx in reversed(order):
        rg_recv(dx).wait_recv()
    rgf[...] = rg[...].astype(F32)

    def chain(n, g, d):
        return n // 2 - (g + d) % 2 if n % 2 == 0 else n // 2

    def y_msg(d, k, g, src):
        to = dev(x, yat(1 if d == 0 else ny - 1), c, z)
        return remote(
            src, ry.at[d, k, group(g)], ys_sem.at[d, k, g], yr_sem.at[d, k, g], to
        )

    def z_msg(d, k, g, src):
        to = dev(x, y, c, zat(1 if d == 0 else nz - 1))
        return remote(
            src, rz.at[d, k, group(g)], zs_sem.at[d, k, g], zr_sem.at[d, k, g], to
        )

    def away(at, n, d, steps):
        return mod(at + steps, n) if d == 0 else mod(at + n - steps, n)

    rings = (
        (ny, y, ty, ry, y_msg),
        (nz, z, tz, rz, z_msg),
    )

    slot_full = lax.broadcasted_iota(jnp.int32, (cap, toks), 0).astype(F32)
    row = lax.broadcasted_iota(jnp.int32, (half, toks), 0)
    slot_half = (div(row, q) * (2 * q) + c * q + mod(row, q)).astype(F32)
    own_row = lax.broadcasted_iota(jnp.int32, (q, toks), 0)
    slot_own = (own_row + (mod(y, yb) * (2 * q) + c * q)).astype(F32)
    own_block = div(y, yb)
    tile = 256 if h % 256 == 0 else 128

    def start_ring(ring, g):
        n, at, term, buf, msg = ring
        for d in (0, 1):
            length = chain(n, g, d)
            if length > 0:
                dest = away(at, n, d, length)
                msg(d, 0, g, term.at[dest, group(g)]).start()

    def make_weight(g):
        hid_copy(g).wait()

        def dispatch(j, _):
            for e in range(per):
                rk = rgf[j, 0, pl.ds(g * per + e, 1), :]
                gt = rgf[j, 1, pl.ds(g * per + e, 1), :]
                mg[e * cap : (e + 1) * cap, :] = jnp.where(rk == slot_full, gt, 0.0).astype(BF)
            scaled = jnp.dot(mg[...], go_all[j, :, mine], preferred_element_type=F32).astype(BF)
            sc[:, pl.ds(pl.multiple_of(j * cap, cap), cap), :] = scaled.reshape(per, cap, width)
            return 0

        def expert(e, _):
            ee = g * per + e
            wpart = lax.dot_general(
                hid[ee].reshape(2 * lanes, h), sc[e], (((0,), (0,)), ((), ())),
                preferred_element_type=F32,
            )
            tz[:, ee] = wpart.astype(BF).reshape(nz, hz, width)
            return 0

        lax.fori_loop(0, nx, dispatch, 0)
        lax.fori_loop(0, per, expert, 0)
        start_ring(rings[1], g)

    def make_hidden(g):
        if g == 0:
            goc_recv(0).wait_recv()
            for dx in reversed(order):
                goc_recv(dx).wait_recv()
        w_copy(g).wait()
        w_recv(g).wait_recv()

        def dispatch(j, _):
            for e in range(per):
                rk = rgf[j, 0, pl.ds(g * per + e, 1), :]
                mh[e * half : (e + 1) * half, :] = jnp.where(rk == slot_half, 1.0, 0.0).astype(BF)
            rows = jnp.dot(mh[...], go_all[j], preferred_element_type=F32).astype(BF)
            dyh[:, pl.ds(pl.multiple_of(j * half, half), half), :] = rows.reshape(
                per, half, 2 * width
            )
            return 0

        def expert(e, _):
            ee = g * per + e
            own_rank = rgf[own_block, 0, pl.ds(ee, 1), :]
            own_gate = rgf[own_block, 1, pl.ds(ee, 1), :]
            picked = jnp.sum(jnp.where(own_rank == slot_own, own_gate, 0.0), axis=1, keepdims=True)
            gcol[ee] = jnp.broadcast_to(picked, (q, 128))
            rows = dyh[e]
            part = jnp.zeros((lanes, 128), F32)
            for s in range(0, h, tile):
                u = lax.dot_general(
                    rows, w2[ee, s : s + tile, :], (((1,), (1,)), ((), ())),
                    preferred_element_type=F32,
                )
                hh = hid[ee, :, c, :, s : s + tile].reshape(lanes, tile).astype(F32)
                prod = u * hh
                for i in range(0, tile, 128):
                    part = part + prod[:, i : i + 128]
                ty[:, ee, :, s : s + tile] = u.astype(BF).reshape(ny, q, tile)
            gall[y, pl.ds(ee, 1), :] = jnp.sum(part.T, axis=0, keepdims=True)
            return 0

        lax.fori_loop(0, nx, dispatch, 0)
        lax.fori_loop(0, per, expert, 0)
        start_ring(rings[0], g)

    def ga_send(dy):
        return remote(
            gall.at[y], gall.at[y], ga_s.at[dy], ga_r.at[dy], dev(x, yat(dy), c, z)
        )

    def ga_recv(dy):
        place = gall.at[yat(ny - dy)]
        return remote(place, place, ga_s.at[dy], ga_r.at[dy], dev(x, yat(dy), c, z))

    def send_gates():
        for dy in range(1, ny):
            ga_send(dy).start()

    offsets = [(dx, r) for dx in range(nx) for r in (0, 1) if dx or r]

    def sg_send(dx, r):
        return remote(
            sgx.at[x, c], sgx.at[x, c], sg_s.at[dx, r], sg_r.at[dx, r],
            dev(xat(dx), y, mod(c + r, 2), z),
        )

    def sg_recv(dx, r):
        place = sgx.at[xat(nx - dx), mod(c + r, 2)]
        return remote(
            place, place, sg_s.at[dx, r], sg_r.at[dx, r], dev(xat(dx), y, mod(c + r, 2), z)
        )

    def sum_gates():
        for dy in range(1, ny):
            ga_recv(dy).wait_recv()
        total = gall[0]
        for i in range(1, ny):
            total = total + gall[i]
        sgx[x, c] = total
        for dx, r in offsets:
            sg_send(dx, r).start()

    def place_gates():
        for dx, r in offsets:
            sg_recv(dx, r).wait_recv()
        for g in range(nx):
            slot = jnp.maximum(rg_send[g, 0].astype(F32), 0.0).astype(jnp.int32)
            lane = (x * yb + div(slot, 2 * q)) * q + mod(slot, q)
            odd = mod(div(slot, q), 2) == 1
            for s in range(0, toks, lanes):
                idx = lane[:, s : s + lanes]
                low = jnp.take_along_axis(sgx[g, 0], idx, axis=1, mode="promise_in_bounds")
                high = jnp.take_along_axis(sgx[g, 1], idx, axis=1, mode="promise_in_bounds")
                gsc[g * experts : (g + 1) * experts, s : s + lanes] = jnp.where(
                    odd[:, s : s + lanes], high, low
                )
        chosen = routes[...]
        out = jnp.zeros((top, toks), F32)
        for e in range(all_experts):
            out = jnp.where(chosen == e, gsc[e : e + 1, :], out)
        gg_out[...] = out

    def add_on(ring, k, g):
        n, at, term, buf, msg = ring
        for d in (0, 1):
            length = chain(n, g, d)
            if k < length:
                place = buf.at[d, k - 1, group(g)]
                msg(d, k - 1, g, place).wait_recv()
                dest = away(at, n, d, length - k)

                def one(e, _):
                    ee = g * per + e
                    held = buf[d, k - 1, ee].astype(F32) + term[dest, ee].astype(F32)
                    buf[d, k - 1, ee] = held.astype(BF)
                    return 0

                lax.fori_loop(0, per, one, 0)
                msg(d, k, g, place).start()

    def finish(ring, g, store):
        n, at, term, buf, msg = ring
        lengths = [chain(n, g, d) for d in (0, 1)]
        for d in (0, 1):
            if lengths[d] > 0:
                msg(d, lengths[d] - 1, g, buf.at[d, lengths[d] - 1, group(g)]).wait_recv()

        def one(e, _):
            ee = g * per + e
            total = term[at, ee].astype(F32)
            for d in (0, 1):
                if lengths[d] > 0:
                    total = total + buf[d, lengths[d] - 1, ee].astype(F32)
            store(total, ee)
            return 0

        lax.fori_loop(0, per, one, 0)

    def store_y(total, g):
        scale = gcol[g]
        for s in range(0, h, 128):
            gh_out[g, :, s : s + 128] = (total[:, s : s + 128] * scale).astype(BF)

    def store_z(total, g):
        gw_out[g] = total.astype(BF)

    for what, ring, k, g in timeline(ny, nz, groups):
        if what == "make":
            (make_hidden, make_weight)[ring](g)
        elif what == "add":
            add_on(rings[ring], k, g)
        elif what == "end":
            finish(rings[ring], g, (store_y, store_z)[ring])
        else:
            (send_gates, sum_gates, place_gates)[k]()

    for g in range(groups):
        w_send(g).wait_send()
        for n, at, term, buf, msg in rings:
            for d in (0, 1):
                for k in range(chain(n, g, d)):
                    msg(d, k, g, term.at[0, group(g)]).wait_send()
    goc_send(0).wait_send()
    for dx in range(1, nx):
        gox_send(dx).wait_send()
        goc_send(dx).wait_send()
        rg_copy(dx).wait_send()
    for dy in range(1, ny):
        ga_send(dy).wait_send()
    for dx, r in offsets:
        sg_send(dx, r).wait_send()


def on_device(nx, ny, nz, groups, grad_out, routes, gates, hidden, w_down):
    experts, slots, h = hidden.shape
    _, toks, width = grad_out.shape
    top = routes.shape[2]
    q = slots // (2 * ny)
    hz = h // nz
    per = experts // groups
    cap = slots // nx
    half = cap // 2
    ky, kz = max(ny // 2, 1), max(nz // 2, 1)
    dma = pltpu.SemaphoreType.DMA
    vmem = pl.BlockSpec(memory_space=pltpu.VMEM)
    anywhere = pl.BlockSpec(memory_space=pl.ANY)
    gh, gw, gg = pl.pallas_call(
        functools.partial(kernel, nx, ny, nz, groups),
        out_shape=(
            jax.ShapeDtypeStruct((experts, q, h), BF),
            jax.ShapeDtypeStruct((experts, hz, width), BF),
            jax.ShapeDtypeStruct((top, toks), F32),
        ),
        in_specs=[anywhere, vmem, vmem, anywhere, anywhere],
        out_specs=(vmem, vmem, vmem),
        scratch_shapes=[
            pltpu.VMEM((experts, ny, 2, q, h), BF),
            pltpu.VMEM((experts, h, 2 * width), BF),
            pltpu.VMEM((nx, toks, 2 * width), BF),
            pltpu.VMEM((nx, 2, experts, toks), BF),
            pltpu.VMEM((nx, 2, experts, toks), BF),
            pltpu.VMEM((per, ny * q, 2 * width), BF),
            pltpu.VMEM((per, slots, width), BF),
            pltpu.VMEM((per * half, toks), BF),
            pltpu.VMEM((per * cap, toks), BF),
            pltpu.VMEM((experts, q, 128), F32),
            pltpu.VMEM((ny, experts, q, h), BF),
            pltpu.VMEM((nz, experts, hz, width), BF),
            pltpu.VMEM((2, ky, experts, q, h), BF),
            pltpu.VMEM((2, kz, experts, hz, width), BF),
            pltpu.VMEM((ny, experts, ny * q), F32),
            pltpu.VMEM((nx, 2, experts, ny * q), F32),
            pltpu.VMEM((nx * experts, toks), F32),
            pltpu.VMEM((nx, 2, experts, toks), F32),
            dma((groups,)),
            dma((groups,)),
            dma((groups,)),
            dma((groups,)),
            dma,
            dma((nx,)),
            dma((nx,)),
            dma((nx,)),
            dma((nx,)),
            dma((nx,)),
            dma((nx,)),
            dma((2, ky, groups)),
            dma((2, ky, groups)),
            dma((2, kz, groups)),
            dma((2, kz, groups)),
            dma((ny,)),
            dma((ny,)),
            dma((nx, 2)),
            dma((nx, 2)),
        ],
        compiler_params=pltpu.CompilerParams(
            collective_id=0, has_side_effects=True, vmem_limit_bytes=58 * 1024 * 1024
        ),
    )(
        grad_out.reshape(toks, width),
        routes.reshape(toks, top).T,
        gates.reshape(toks, top).T,
        hidden.reshape(experts, ny, 2, q, h),
        w_down,
    )
    return gh, gw, gg.T.reshape(1, toks, top)


def solution(mesh):
    nx, ny, nz = mesh.shape["expert"], mesh.shape["tensor"] // 2, mesh.shape["dp"]
    groups = 4
    placed = (
        P("dp", "expert", "tensor"),
        P("dp", "expert", None),
        P("dp", "expert", None),
        P("expert", "dp", None),
        P("expert", None, "tensor"),
    )
    return jax.shard_map(
        functools.partial(on_device, nx, ny, nz, groups),
        mesh=mesh,
        in_specs=placed,
        out_specs=(
            P("expert", ("dp", "tensor"), None),
            P("expert", "dp", "tensor"),
            P("dp", "expert", None),
        ),
        check_vma=False,
    )
```

```python
import functools
import heapq

import jax
import jax.numpy as jnp
from jax import lax
from jax.experimental import pallas as pl
from jax.experimental.pallas import tpu as pltpu
from jax.sharding import PartitionSpec as P

MESH = pl.DeviceIdType.MESH
BF = jnp.bfloat16
F32 = jnp.float32


def mod(a, n):
    return lax.rem(a, jnp.int32(n))


def div(a, n):
    return lax.div(a, jnp.int32(n))


def timeline(ny, nz, groups):
    size = {0: 8.8 / groups, 1: 5.8 / groups}
    steps = {0: ny // 2, 1: nz // 2}
    work = {"make": 5.4 / groups, "add": 1.6 / groups}
    latency = 1.8
    makes = [(r, g) for g in range(groups) for r in (1, 0)]
    free = {0: 0.0, 1: 0.0}
    ready, order, now, gate = [], [], 0.0, None

    def send(r, k, g, at):
        free[r] = max(free[r], at) + size[r]
        heapq.heappush(ready, (free[r] + latency, r, k + 1, g))

    while makes or ready or gate:
        if gate and gate[0] <= now:
            order.append(("gate", 0, gate[1], 0))
            now += 0.3
            gate = (now + 6.0, gate[1] + 1) if gate[1] < 2 else None
        elif ready and (ready[0][0] <= now or not makes):
            arrived, r, k, g = heapq.heappop(ready)
            now = max(now, arrived) + work["add"]
            order.append(("end" if k == steps[r] else "add", r, k, g))
            if k < steps[r]:
                send(r, k, g, now)
        elif makes:
            r, g = makes.pop(0)
            now += work["make"]
            order.append(("make", r, 0, g))
            send(r, 0, g, now)
            if not makes:
                gate = (now, 0)
        else:
            now = gate[0]
    return order


def kernel(
    nx, ny, nz, groups,
    go_in, routes, gates, hid_in, w_in,
    gh_out, gw_out, gg_out,
    hid, w2, go_all, rg_send, rg, dyh, sc, mh, mg, gcol,
    ty, tz, ry, rz, gall, sgx, gsc, rgf,
    hid_sem, wl_sem, ws_sem, wr_sem, go_l, gox_s, gox_r, goc_s, goc_r, rg_s, rg_r,
    ys_sem, yr_sem, zs_sem, zr_sem, ga_s, ga_r, sg_s, sg_r,
):
    top, toks = routes.shape
    width = go_in.shape[1]
    experts, _, _, q, h = hid.shape
    per = experts // groups
    cap = 2 * ny * q // nx
    yb = ny // nx
    half = yb * q
    hz = h // nz
    lanes = ny * q
    x = lax.axis_index("expert")
    t = lax.axis_index("tensor")
    z = lax.axis_index("dp")
    y = div(t, 2)
    c = mod(t, 2)
    peer_c = 1 - c

    def dev(xx, yy, cc, zz):
        return {"expert": xx, "tensor": yy * 2 + cc, "dp": zz}

    def xat(dx):
        return mod(x + dx, nx)

    def yat(dy):
        return mod(y + dy, ny)

    def zat(dz):
        return mod(z + dz, nz)

    peer = dev(x, y, peer_c, z)

    def remote(src, dst, ssem, rsem, to):
        return pltpu.make_async_remote_copy(
            src_ref=src, dst_ref=dst, send_sem=ssem, recv_sem=rsem,
            device_id=to, device_id_type=MESH,
        )

    barrier = pltpu.get_barrier_semaphore()
    partners = [peer]
    partners += [dev(xat(dx), y, mod(c + r, 2), z) for dx in range(1, nx) for r in (0, 1)]
    partners += [dev(x, yat(dy), c, z) for dy in range(1, ny)]
    partners += [dev(x, y, c, zat(dz)) for dz in sorted({1, nz - 1})]
    for partner in partners:
        pl.semaphore_signal(barrier, inc=1, device_id=partner, device_id_type=MESH)

    mine = pl.ds(pl.multiple_of(c * width, width), width)
    others = pl.ds(pl.multiple_of(peer_c * width, width), width)

    def group(g):
        return pl.ds(g * per, per)

    go_local = pltpu.make_async_copy(go_in, go_all.at[x, :, mine], go_l)
    go_local.start()

    def hid_copy(g):
        return pltpu.make_async_copy(hid_in.at[group(g)], hid.at[group(g)], hid_sem.at[g])

    def w_copy(g):
        return pltpu.make_async_copy(w_in.at[group(g)], w2.at[group(g), :, mine], wl_sem.at[g])

    def w_send(g):
        return remote(w_in.at[group(g)], w2.at[group(g), :, mine], ws_sem.at[g], wr_sem.at[g], peer)

    def w_recv(g):
        place = w2.at[group(g), :, others]
        return remote(place, place, ws_sem.at[g], wr_sem.at[g], peer)

    for g in range(groups):
        w_copy(g).start()
        hid_copy(g).start()

    pl.semaphore_wait(barrier, len(partners))

    def gox_send(dx):
        return remote(
            go_in, go_all.at[x, :, mine], gox_s.at[dx], gox_r.at[dx], dev(xat(dx), y, c, z)
        )

    def gox_recv(dx):
        place = go_all.at[xat(nx - dx), :, mine]
        return remote(place, place, gox_s.at[dx], gox_r.at[dx], dev(xat(dx), y, c, z))

    def goc_send(dx):
        src = xat(nx - dx)
        place = go_all.at[src, :, mine]
        return remote(place, place, goc_s.at[dx], goc_r.at[dx], peer)

    def goc_recv(dx):
        place = go_all.at[xat(nx - dx), :, others]
        return remote(place, place, goc_s.at[dx], goc_r.at[dx], peer)

    def rg_copy(dx):
        to = xat(dx)
        return remote(
            rg_send.at[to], rg.at[x], rg_s.at[dx], rg_r.at[dx], dev(to, y, c, z)
        )

    def rg_recv(dx):
        place = rg.at[xat(nx - dx)]
        return remote(place, place, rg_s.at[dx], rg_r.at[dx], dev(xat(dx), y, c, z))

    order = sorted(range(1, nx), key=lambda dx: -min(dx, nx - dx))
    for dx in order:
        gox_send(dx).start()
    go_local.wait()
    goc_send(0).start()
    for g in range(groups):
        w_send(g).start()

    all_experts = nx * experts
    eidx = lax.broadcasted_iota(jnp.int32, (all_experts, toks), 0)
    hot = jnp.zeros((all_experts, toks), F32)
    weight = jnp.zeros((all_experts, toks), F32)
    gf = gates[...].astype(F32)
    rt = routes[...]
    for k in range(top):
        named = rt[k : k + 1, :] == eidx
        hot = jnp.where(named, 1.0, hot)
        weight = jnp.where(named, gf[k : k + 1, :], weight)
    before = lax.broadcasted_iota(jnp.int32, (toks, toks), 0) < lax.broadcasted_iota(
        jnp.int32, (toks, toks), 1
    )
    rank = jnp.dot(hot.astype(BF), before.astype(F32).astype(BF), preferred_element_type=F32)
    rank = jnp.where(hot > 0.5, rank, -1.0)
    for g in range(nx):
        rg_send[g, 0] = rank[g * experts : (g + 1) * experts].astype(BF)
        rg_send[g, 1] = weight[g * experts : (g + 1) * experts].astype(BF)
    rg[x] = rg_send[x]
    for dx in order:
        rg_copy(dx).start()
    for dx in reversed(order):
        gox_recv(dx).wait_recv()
        goc_send(dx).start()
    for dx in reversed(order):
        rg_recv(dx).wait_recv()
    rgf[...] = rg[...].astype(F32)

    def chain(n, g, d):
        return n // 2 - (g + d) % 2 if n % 2 == 0 else n // 2

    def y_msg(d, k, g, src):
        to = dev(x, yat(1 if d == 0 else ny - 1), c, z)
        return remote(
            src, ry.at[d, k, group(g)], ys_sem.at[d, k, g], yr_sem.at[d, k, g], to
        )

    def z_msg(d, k, g, src):
        to = dev(x, y, c, zat(1 if d == 0 else nz - 1))
        return remote(
            src, rz.at[d, k, group(g)], zs_sem.at[d, k, g], zr_sem.at[d, k, g], to
        )

    def away(at, n, d, steps):
        return mod(at + steps, n) if d == 0 else mod(at + n - steps, n)

    rings = (
        (ny, y, ty, ry, y_msg),
        (nz, z, tz, rz, z_msg),
    )

    slot_full = lax.broadcasted_iota(jnp.int32, (cap, toks), 0).astype(F32)
    row = lax.broadcasted_iota(jnp.int32, (half, toks), 0)
    slot_half = (div(row, q) * (2 * q) + c * q + mod(row, q)).astype(F32)
    own_row = lax.broadcasted_iota(jnp.int32, (q, toks), 0)
    slot_own = (own_row + (mod(y, yb) * (2 * q) + c * q)).astype(F32)
    own_block = div(y, yb)
    tile = 256 if h % 256 == 0 else 128

    def start_ring(ring, g):
        n, at, term, buf, msg = ring
        for d in (0, 1):
            length = chain(n, g, d)
            if length > 0:
                dest = away(at, n, d, length)
                msg(d, 0, g, term.at[dest, group(g)]).start()

    def make_weight(g):
        hid_copy(g).wait()

        def dispatch(j, _):
            for e in range(per):
                rk = rgf[j, 0, pl.ds(g * per + e, 1), :]
                gt = rgf[j, 1, pl.ds(g * per + e, 1), :]
                mg[e * cap : (e + 1) * cap, :] = jnp.where(rk == slot_full, gt, 0.0).astype(BF)
            scaled = jnp.dot(mg[...], go_all[j, :, mine], preferred_element_type=F32).astype(BF)
            sc[:, pl.ds(pl.multiple_of(j * cap, cap), cap), :] = scaled.reshape(per, cap, width)
            return 0

        def expert(e, _):
            ee = g * per + e
            wpart = lax.dot_general(
                hid[ee].reshape(2 * lanes, h), sc[e], (((0,), (0,)), ((), ())),
                preferred_element_type=F32,
            )
            tz[:, ee] = wpart.astype(BF).reshape(nz, hz, width)
            return 0

        lax.fori_loop(0, nx, dispatch, 0)
        lax.fori_loop(0, per, expert, 0)
        start_ring(rings[1], g)

    def make_hidden(g):
        if g == 0:
            goc_recv(0).wait_recv()
            for dx in reversed(order):
                goc_recv(dx).wait_recv()
        w_copy(g).wait()
        w_recv(g).wait_recv()

        def dispatch(j, _):
            for e in range(per):
                rk = rgf[j, 0, pl.ds(g * per + e, 1), :]
                mh[e * half : (e + 1) * half, :] = jnp.where(rk == slot_half, 1.0, 0.0).astype(BF)
            rows = jnp.dot(mh[...], go_all[j], preferred_element_type=F32).astype(BF)
            dyh[:, pl.ds(pl.multiple_of(j * half, half), half), :] = rows.reshape(
                per, half, 2 * width
            )
            return 0

        def expert(e, _):
            ee = g * per + e
            own_rank = rgf[own_block, 0, pl.ds(ee, 1), :]
            own_gate = rgf[own_block, 1, pl.ds(ee, 1), :]
            picked = jnp.sum(jnp.where(own_rank == slot_own, own_gate, 0.0), axis=1, keepdims=True)
            gcol[ee] = jnp.broadcast_to(picked, (q, 128))
            rows = dyh[e]
            part = jnp.zeros((lanes, 128), F32)
            for s in range(0, h, tile):
                u = lax.dot_general(
                    rows, w2[ee, s : s + tile, :], (((1,), (1,)), ((), ())),
                    preferred_element_type=F32,
                )
                hh = hid[ee, :, c, :, s : s + tile].reshape(lanes, tile).astype(F32)
                prod = u * hh
                for i in range(0, tile, 128):
                    part = part + prod[:, i : i + 128]
                ty[:, ee, :, s : s + tile] = u.astype(BF).reshape(ny, q, tile)
            gall[y, pl.ds(ee, 1), :] = jnp.sum(part.T, axis=0, keepdims=True)
            return 0

        lax.fori_loop(0, nx, dispatch, 0)
        lax.fori_loop(0, per, expert, 0)
        start_ring(rings[0], g)

    def ga_send(dy):
        return remote(
            gall.at[y], gall.at[y], ga_s.at[dy], ga_r.at[dy], dev(x, yat(dy), c, z)
        )

    def ga_recv(dy):
        place = gall.at[yat(ny - dy)]
        return remote(place, place, ga_s.at[dy], ga_r.at[dy], dev(x, yat(dy), c, z))

    def send_gates():
        for dy in range(1, ny):
            ga_send(dy).start()

    offsets = [(dx, r) for dx in range(nx) for r in (0, 1) if dx or r]

    def sg_send(dx, r):
        return remote(
            sgx.at[x, c], sgx.at[x, c], sg_s.at[dx, r], sg_r.at[dx, r],
            dev(xat(dx), y, mod(c + r, 2), z),
        )

    def sg_recv(dx, r):
        place = sgx.at[xat(nx - dx), mod(c + r, 2)]
        return remote(
            place, place, sg_s.at[dx, r], sg_r.at[dx, r], dev(xat(dx), y, mod(c + r, 2), z)
        )

    def sum_gates():
        for dy in range(1, ny):
            ga_recv(dy).wait_recv()
        total = gall[0]
        for i in range(1, ny):
            total = total + gall[i]
        sgx[x, c] = total
        for dx, r in offsets:
            sg_send(dx, r).start()

    def place_gates():
        for dx, r in offsets:
            sg_recv(dx, r).wait_recv()
        for g in range(nx):
            slot = jnp.maximum(rg_send[g, 0].astype(F32), 0.0).astype(jnp.int32)
            lane = (x * yb + div(slot, 2 * q)) * q + mod(slot, q)
            odd = mod(div(slot, q), 2) == 1
            for s in range(0, toks, lanes):
                idx = lane[:, s : s + lanes]
                low = jnp.take_along_axis(sgx[g, 0], idx, axis=1, mode="promise_in_bounds")
                high = jnp.take_along_axis(sgx[g, 1], idx, axis=1, mode="promise_in_bounds")
                gsc[g * experts : (g + 1) * experts, s : s + lanes] = jnp.where(
                    odd[:, s : s + lanes], high, low
                )
        chosen = routes[...]
        out = jnp.zeros((top, toks), F32)
        for e in range(all_experts):
            out = jnp.where(chosen == e, gsc[e : e + 1, :], out)
        gg_out[...] = out
        for g in range(groups):
            w_send(g).wait_send()
        goc_send(0).wait_send()
        for dx in range(1, nx):
            gox_send(dx).wait_send()
            goc_send(dx).wait_send()
            rg_copy(dx).wait_send()
        for dy in range(1, ny):
            ga_send(dy).wait_send()

    def left(ring, k, g):
        n, at, term, buf, msg = ring
        for d in (0, 1):
            if k - 1 < chain(n, g, d):
                msg(d, k - 1, g, term.at[0, group(g)]).wait_send()

    def add_on(ring, k, g):
        n, at, term, buf, msg = ring
        for d in (0, 1):
            length = chain(n, g, d)
            if k < length:
                place = buf.at[d, k - 1, group(g)]
                msg(d, k - 1, g, place).wait_recv()
                dest = away(at, n, d, length - k)

                def one(e, _):
                    ee = g * per + e
                    held = buf[d, k - 1, ee].astype(F32) + term[dest, ee].astype(F32)
                    buf[d, k - 1, ee] = held.astype(BF)
                    return 0

                lax.fori_loop(0, per, one, 0)
                msg(d, k, g, place).start()
        left(ring, k, g)

    def finish(ring, g, store):
        n, at, term, buf, msg = ring
        lengths = [chain(n, g, d) for d in (0, 1)]
        for d in (0, 1):
            if lengths[d] > 0:
                msg(d, lengths[d] - 1, g, buf.at[d, lengths[d] - 1, group(g)]).wait_recv()

        def one(e, _):
            ee = g * per + e
            total = term[at, ee].astype(F32)
            for d in (0, 1):
                if lengths[d] > 0:
                    total = total + buf[d, lengths[d] - 1, ee].astype(F32)
            store(total, ee)
            return 0

        lax.fori_loop(0, per, one, 0)
        left(ring, n // 2, g)

    def store_y(total, g):
        scale = gcol[g]
        for s in range(0, h, 128):
            gh_out[g, :, s : s + 128] = (total[:, s : s + 128] * scale).astype(BF)

    def store_z(total, g):
        gw_out[g] = total.astype(BF)

    for what, ring, k, g in timeline(ny, nz, groups):
        if what == "make":
            (make_hidden, make_weight)[ring](g)
        elif what == "add":
            add_on(rings[ring], k, g)
        elif what == "end":
            finish(rings[ring], g, (store_y, store_z)[ring])
        else:
            (send_gates, sum_gates, place_gates)[k]()

    for dx, r in offsets:
        sg_send(dx, r).wait_send()


def on_device(nx, ny, nz, groups, grad_out, routes, gates, hidden, w_down):
    experts, slots, h = hidden.shape
    _, toks, width = grad_out.shape
    top = routes.shape[2]
    q = slots // (2 * ny)
    hz = h // nz
    per = experts // groups
    cap = slots // nx
    half = cap // 2
    ky, kz = max(ny // 2, 1), max(nz // 2, 1)
    dma = pltpu.SemaphoreType.DMA
    vmem = pl.BlockSpec(memory_space=pltpu.VMEM)
    anywhere = pl.BlockSpec(memory_space=pl.ANY)
    gh, gw, gg = pl.pallas_call(
        functools.partial(kernel, nx, ny, nz, groups),
        out_shape=(
            jax.ShapeDtypeStruct((experts, q, h), BF),
            jax.ShapeDtypeStruct((experts, hz, width), BF),
            jax.ShapeDtypeStruct((top, toks), F32),
        ),
        in_specs=[anywhere, vmem, vmem, anywhere, anywhere],
        out_specs=(vmem, vmem, vmem),
        scratch_shapes=[
            pltpu.VMEM((experts, ny, 2, q, h), BF),
            pltpu.VMEM((experts, h, 2 * width), BF),
            pltpu.VMEM((nx, toks, 2 * width), BF),
            pltpu.VMEM((nx, 2, experts, toks), BF),
            pltpu.VMEM((nx, 2, experts, toks), BF),
            pltpu.VMEM((per, ny * q, 2 * width), BF),
            pltpu.VMEM((per, slots, width), BF),
            pltpu.VMEM((per * half, toks), BF),
            pltpu.VMEM((per * cap, toks), BF),
            pltpu.VMEM((experts, q, 128), F32),
            pltpu.VMEM((ny, experts, q, h), BF),
            pltpu.VMEM((nz, experts, hz, width), BF),
            pltpu.VMEM((2, ky, experts, q, h), BF),
            pltpu.VMEM((2, kz, experts, hz, width), BF),
            pltpu.VMEM((ny, experts, ny * q), F32),
            pltpu.VMEM((nx, 2, experts, ny * q), F32),
            pltpu.VMEM((nx * experts, toks), F32),
            pltpu.VMEM((nx, 2, experts, toks), F32),
            dma((groups,)),
            dma((groups,)),
            dma((groups,)),
            dma((groups,)),
            dma,
            dma((nx,)),
            dma((nx,)),
            dma((nx,)),
            dma((nx,)),
            dma((nx,)),
            dma((nx,)),
            dma((2, ky, groups)),
            dma((2, ky, groups)),
            dma((2, kz, groups)),
            dma((2, kz, groups)),
            dma((ny,)),
            dma((ny,)),
            dma((nx, 2)),
            dma((nx, 2)),
        ],
        compiler_params=pltpu.CompilerParams(
            collective_id=0, has_side_effects=True, vmem_limit_bytes=58 * 1024 * 1024
        ),
    )(
        grad_out.reshape(toks, width),
        routes.reshape(toks, top).T,
        gates.reshape(toks, top).T,
        hidden.reshape(experts, ny, 2, q, h),
        w_down,
    )
    return gh, gw, gg.T.reshape(1, toks, top)


def solution(mesh):
    nx, ny, nz = mesh.shape["expert"], mesh.shape["tensor"] // 2, mesh.shape["dp"]
    groups = 4
    placed = (
        P("dp", "expert", "tensor"),
        P("dp", "expert", None),
        P("dp", "expert", None),
        P("expert", "dp", None),
        P("expert", None, "tensor"),
    )
    return jax.shard_map(
        functools.partial(on_device, nx, ny, nz, groups),
        mesh=mesh,
        in_specs=placed,
        out_specs=(
            P("expert", ("dp", "tensor"), None),
            P("expert", "dp", "tensor"),
            P("dp", "expert", None),
        ),
        check_vma=False,
    )
```
